128 devices in a mesh: row: 8 (over y, x_lo), col: 16 (over x_hi, z, core).
Axes of the slice: x: 4 (x_hi: 2, x_lo: 2; x = x_hi * 2 + x_lo), y: 4, z: 4, core: 2. Of those that a mesh axis runs over, the one named last changes fastest.
Arguments:
- homolog_features: bfloat16 [128, 2048, 64], P('col', 'row'), may hold values from -6 to 6
- validity_indicator: int32 [128, 64], P('col', 'row'), may hold values from -2147483648 to 2147483647, as said below
- standardize_scaling: float32 [64], replicated, may hold values from 0.1 to 1.9
- source_projector: bfloat16 [64, 32], replicated, may hold values from -0.75 to 0.75
- target_projector: bfloat16 [64, 32], replicated, may hold values from -0.75 to 0.75
- final_projector: bfloat16 [1024, 128], replicated, may hold values from -0.75 to 0.75
- final_offset: float32 [128], replicated, may hold values from -3 to 3
Outputs:
- pair_update: bfloat16 [2048, 2048, 128], P('row', 'col')
The draws below stay inside these ranges and needn't reach their ends.
Inputs may be any that keep to these rules, and one draw needn't show every extreme that they name: `validity_indicator`: bit k of word w of sequence s is the mask of residue 32 * w + k; some residues are masked in every sequence.
All inputs are finite; a program needn't handle non-finite values.
Results may differ from the reference program's by a relative error of at most 0.0069.
Values may be sent and summed in bfloat16 or wider, within the bound.
A program may use at most 128 MiB of HBM per device.

```python
import jax
import jax.numpy as jnp
from jax import lax

FEATURE_DEPTH = 64
PROJECTED_WIDTH = 32
CZ = 128
HOMOLOG_COUNT = 128
WINDOW_POSITIONS = 2048


def draw_validity_indicator(key, part):
    key = jax.random.fold_in(key, 7)
    level_key, random_seed_entry = jax.random.split(key)
    residue_level = jax.random.randint(level_key, (1, WINDOW_POSITIONS), 0, 9)
    grid_entries = jax.random.randint(random_seed_entry, (HOMOLOG_COUNT, WINDOW_POSITIONS), 0, 8)
    bit_values = (grid_entries < residue_level).astype(jnp.int32).reshape(HOMOLOG_COUNT, WINDOW_POSITIONS // 32, 32)
    shifts = jnp.arange(32, dtype=jnp.int32)
    return jnp.sum(jnp.left_shift(bit_values, shifts), axis=-1, dtype=jnp.int32)


def draw_homolog_features(key, part):
    key = jax.random.fold_in(key, 11)
    value_key, pick_key, level_key = jax.random.split(key, 3)
    full_shape = (HOMOLOG_COUNT, WINDOW_POSITIONS, FEATURE_DEPTH)
    values = jnp.clip(jax.random.normal(value_key, full_shape, jnp.float32), -6.0, 6.0)
    flat_rows = jax.random.randint(pick_key, (HOMOLOG_COUNT, WINDOW_POSITIONS, 1), 0, 16) == 0
    constant = jax.random.uniform(level_key, (HOMOLOG_COUNT, WINDOW_POSITIONS, 1), jnp.float32, -6.0, 6.0)
    return jnp.where(flat_rows, constant, values).astype(jnp.bfloat16)


def bell_draw(stream_key, extent, scale, most, kind=jnp.bfloat16):
    values = scale * jax.random.normal(stream_key, extent, jnp.float32)
    return jnp.clip(values, min=-most, max=most).astype(kind)


def setup_inputs(seed: int = 0) -> dict:
    key_list = jax.random.split(jax.random.key(seed), 8)
    homolog_features = draw_homolog_features(jax.random.fold_in(key_list[7], 71), 0)
    validity_indicator = draw_validity_indicator(jax.random.fold_in(key_list[7], 71), 0)
    standardize_scaling = jnp.clip(1.0 + 0.18 * jax.random.normal(key_list[2], (FEATURE_DEPTH,), jnp.float32), 0.1, 1.9)
    source_projector = bell_draw(key_list[3], (FEATURE_DEPTH, PROJECTED_WIDTH), FEATURE_DEPTH ** -0.5, 0.75)
    target_projector = bell_draw(key_list[4], (FEATURE_DEPTH, PROJECTED_WIDTH), FEATURE_DEPTH ** -0.5, 0.75)
    final_projector = bell_draw(key_list[5], (PROJECTED_WIDTH * PROJECTED_WIDTH, CZ), (PROJECTED_WIDTH * PROJECTED_WIDTH // 16) ** -0.5, 0.75)
    final_offset = bell_draw(key_list[6], (CZ,), 0.5, 3.0, jnp.float32)
    return {"homolog_features": homolog_features, "validity_indicator": validity_indicator, "standardize_scaling": standardize_scaling, "source_projector": source_projector, "target_projector": target_projector, "final_projector": final_projector, "final_offset": final_offset}


def unpack_mask(packed_words):
    positions = jnp.arange(32, dtype=jnp.int32)
    bit_values = jnp.bitwise_and(jnp.right_shift(packed_words[..., None], positions), 1)
    return bit_values.reshape(packed_words.shape[0], packed_words.shape[1] * 32)

def tensor_couples(homolog_features, mask_values, standardize_scaling, source_projector, target_projector):
    tensor_products = homolog_features.astype(jnp.float32)
    center = lax.optimization_barrier(jnp.mean(tensor_products, axis=-1, keepdims=True))
    spread = lax.optimization_barrier(jnp.mean((tensor_products - center) ** 2, axis=-1, keepdims=True))
    normed = ((tensor_products - center) * lax.rsqrt(spread + 1e-05) * standardize_scaling).astype(jnp.bfloat16)
    weight_matrix = mask_values.astype(jnp.float32)[..., None]
    source_embedding = (jnp.einsum('srm,mh->srh', normed, source_projector, preferred_element_type=jnp.float32) * weight_matrix).astype(jnp.bfloat16)
    target_embedding = (jnp.einsum('srm,mh->srh', normed, target_projector, preferred_element_type=jnp.float32) * weight_matrix).astype(jnp.bfloat16)
    return (source_embedding, target_embedding)

def reference(homolog_features, validity_indicator, standardize_scaling, source_projector, target_projector, final_projector, final_offset):
    mask_values = unpack_mask(validity_indicator)
    source_embedding, target_embedding = tensor_couples(homolog_features, mask_values, standardize_scaling, source_projector, target_projector)
    mask_float = mask_values.astype(jnp.float32)
    counts = jnp.dot(mask_float.T, mask_float, preferred_element_type=jnp.float32)
    denom = jnp.maximum(counts, 1.0)
    tiles_list = WINDOW_POSITIONS // 16
    source_tiles = source_embedding.reshape(HOMOLOG_COUNT, tiles_list, 16, PROJECTED_WIDTH).transpose(1, 0, 2, 3)
    denom_blocks = denom.reshape(tiles_list, 16, WINDOW_POSITIONS)

    def one_block(args):
        piece, scale = args
        outer = jnp.einsum('sic,sje->ijce', piece.astype(jnp.float32), target_embedding.astype(jnp.float32))
        outer = outer.astype(jnp.bfloat16).reshape(16 * WINDOW_POSITIONS, PROJECTED_WIDTH * PROJECTED_WIDTH)
        projected = jnp.dot(outer, final_projector, preferred_element_type=jnp.float32).reshape(16, WINDOW_POSITIONS, CZ)
        return (projected / scale[..., None] + final_offset).astype(jnp.bfloat16)
    result = lax.map(one_block, (source_tiles, denom_blocks))
    return result.reshape(WINDOW_POSITIONS, WINDOW_POSITIONS, CZ)
```

```python
import functools

import jax
import jax.numpy as jnp
from jax import lax
from jax.experimental import pallas as pl
from jax.experimental.pallas import tpu as pltpu
from jax.sharding import PartitionSpec as P

BF16 = jnp.bfloat16
F32 = jnp.float32
MESH = pl.DeviceIdType.MESH

SEQS = 8
ROWS = 256
COLS = 128
WIDTH = 32
DEPTH = 64
CZ = 128
SLOTS = 16
PARTS = 4
L_ROWS = 16 + ROWS // 4 * SEQS
R_ROWS = 16 + WIDTH * SEQS
L_STEP = (L_ROWS - 16) // PARTS
R_STEP = (R_ROWS - 16) // PARTS


def span(step, part):
    return pl.ds(0, 16 + step) if part == 0 else pl.ds(16 + step * part, step)


class Place:
    def __init__(self):
        self.row = lax.axis_index("row")
        self.col = lax.axis_index("col")
        self.y, self.xl = self.row // 2, self.row % 2
        chip = self.col // 2
        self.xh, self.z, self.core = chip // 4, chip % 4, self.col % 2
        self.slot = self.z * 4 + self.xh * 2 + self.core
        self.to_xh, self.to_z = self.y // 2, self.row % 4
        self.relay_y = (self.y + self.z - self.to_z + 4) % 4
        self.from_y, self.from_xl = self.xh * 2 + self.z // 2, self.z % 2

    def near_z(self, y):
        return (y - self.from_y + self.z + 8) % 4

    def device(self, y=None, xl=None, xh=None, z=None, core=None):
        pick = lambda a, b: b if a is None else a
        y, xl, xh = pick(y, self.y), pick(xl, self.xl), pick(xh, self.xh)
        z, core = pick(z, self.z), pick(core, self.core)
        return (y * 2 + xl, (xh * 4 + z) * 2 + core)

    def is_me(self, device):
        return (device[0] == self.row) & (device[1] == self.col)


def normalise(xv, gain_ref, ns, nt):
    gain = jnp.broadcast_to(gain_ref[...], (ROWS, DEPTH)).T
    for s in range(SEQS):
        x = xv[s].astype(F32)
        center = jnp.mean(x, axis=0, keepdims=True)
        d = x - center
        spread = jnp.mean(d * d, axis=0, keepdims=True)
        normed = d * lax.rsqrt(spread + 1e-05) * gain
        nt[s] = normed.astype(BF16)
        ns[pl.ds(s * ROWS, ROWS), :] = normed.T


def masks_by_half(v):
    lane = lax.broadcasted_iota(jnp.int32, (SEQS, 128), 1)
    out = []
    for h in range(2):
        word = jnp.broadcast_to(v[:, 4 * h : 4 * h + 1], (SEQS, 128))
        for q in range(1, 4):
            word = jnp.where(lane // 32 == q, v[:, 4 * h + q : 4 * h + q + 1], word)
        out.append((lax.shift_right_logical(word, lane % 32) & 1).astype(F32))
    return out


def project_right(nt, pt_ref, masks, rs, rsend):
    for s in range(SEQS):
        y = jnp.dot(pt_ref[...], nt[s], preferred_element_type=F32)
        for h in range(2):
            rs[h, pl.ds(s, WIDTH, stride=SEQS), :] = y[:, h * COLS : (h + 1) * COLS]
    tile = jnp.concatenate(masks, axis=0).astype(BF16)
    for h in range(2):
        rsend[h, 0:16, :] = tile
        block = rs[h].reshape(WIDTH, SEQS, COLS) * masks[h][None]
        rsend[h, 16:R_ROWS, :] = block.reshape(WIDTH * SEQS, COLS).astype(BF16)


def project_left(ns, ps_ref, v, masks, lbuf, slot):
    total = None
    p = ps_ref[...].astype(F32).T.astype(BF16)
    zero = jnp.zeros_like(p)
    for a in range(4):
        n = jnp.concatenate(
            [ns[pl.ds(4 * b + a, SEQS, stride=ROWS), :] for b in range(ROWS // 4)], axis=0
        ).astype(BF16)
        wide = jnp.concatenate([p if q == a else zero for q in range(4)], axis=1)
        part = jnp.dot(n, wide, preferred_element_type=F32)
        total = part if total is None else total + part
    shift = lax.broadcasted_iota(jnp.int32, (SEQS, 128), 1) // 32
    mask = []
    for b in range(ROWS // 4):
        word = jnp.broadcast_to(v[:, b // 8 : b // 8 + 1], (SEQS, 128))
        mask.append((lax.shift_right_logical(word, shift + (b % 8) * 4) & 1).astype(F32))
    out = total * jnp.concatenate(mask, axis=0)
    lbuf[slot, 0:16, :] = jnp.concatenate(masks, axis=0).astype(BF16)
    lbuf[slot, 16:L_ROWS, :] = out.astype(BF16)


def reorder_final(wv, wf, wt):
    wf[...] = wv[...].astype(F32)
    for part in range(8):
        rows = [wf[pl.ds(4 * part + e, WIDTH, stride=WIDTH), :] for e in range(4)]
        wt[:, part * 128 : (part + 1) * 128] = jnp.concatenate(rows, axis=0).astype(BF16).T


def unpack_left(lbuf, a_ref, part):
    block = lbuf[:, 16 + L_STEP * part : 16 + L_STEP * (part + 1), :].astype(F32)
    groups = L_STEP // SEQS
    block = block.reshape(SLOTS, groups, SEQS, 128)
    for b in range(groups):
        tile = block[:, b].reshape(SLOTS * SEQS, 128).astype(BF16)
        a_ref[pl.ds((part * groups + b) * 128, 128), :] = tile.T


def unpack_right(rbuf, r_ref, part):
    block = rbuf[:, 16 + R_STEP * part : 16 + R_STEP * (part + 1), :].astype(F32)
    groups = R_STEP // SEQS
    block = block.reshape(SLOTS, groups, SEQS, COLS)
    for e in range(groups):
        at = (part * groups + e) * COLS
        r_ref[:, at : at + COLS] = block[:, e].reshape(SLOTS * SEQS, COLS).astype(BF16)


def count_pairs(lbuf, rbuf, core, rc_ref):
    mi = lbuf[:, 0:16, :].astype(F32).reshape(SLOTS, 2, SEQS, 128)
    mj = rbuf[:, 0:16, :].astype(F32).reshape(SLOTS, 2, SEQS, 128)
    first = (core == 0).astype(F32)
    cols = (mj[:, 0] * first + mj[:, 1] * (1.0 - first)).reshape(128, 128).astype(BF16)
    for h in range(2):
        rows = mi[:, h].reshape(128, 128).astype(BF16)
        counts = lax.dot_general(rows, cols, (((0,), (0,)), ((), ())), preferred_element_type=F32)
        rc_ref[pl.ds(h * 128, 128), :] = 1.0 / jnp.maximum(counts, 1.0)


def gather_kernel(
    x_hbm, v_ref, gain_ref, ps_ref, pt_ref, w_hbm, off_ref,
    a_ref, r_ref, wt_ref, rc_ref, ob_ref,
    xv, wv, wf, ns, nt, rs, rsend, lbuf, rbuf,
    in_sem, rs1, rr1, rs2, rr2, ls, lr, fs, fr,
):
    me = Place()
    x_copy = pltpu.make_async_copy(x_hbm, xv, in_sem.at[0])
    w_copy = pltpu.make_async_copy(w_hbm, wv, in_sem.at[1])
    x_copy.start()
    w_copy.start()

    shifts = [(a, b) for a in range(2) for b in range(4) if (a, b) != (0, 0)]
    partner = me.device(core=1 - me.core)
    aways = [me.device(xh=(me.xh + a) % 2, z=(me.z + b) % 4) for a, b in shifts]
    froms = [((me.xh + a) % 2, (me.z + 4 - b) % 4) for a, b in shifts]
    relays = [
        (h, me.device(y=me.relay_y, xl=xl, xh=me.to_xh, z=me.to_z, core=h))
        for h in range(2) for xl in range(2)
    ]
    near = me.near_z(me.y)
    sources = [
        me.device(y=me.from_y, xl=me.from_xl, xh=xh, z=near, core=c)
        for xh in range(2) for c in range(2)
    ]
    others = [me.device(y=(me.y + d) % 4) for d in (1, 2, 3)]
    bar = pltpu.get_barrier_semaphore()
    friends = aways + [partner] + [d for _, d in relays] + sources + others
    for device in friends:
        pl.semaphore_signal(bar, inc=1, device_id=device, device_id_type=MESH)

    x_copy.wait()
    v = v_ref[...]
    masks = masks_by_half(v)
    normalise(xv, gain_ref, ns, nt)
    project_right(nt, pt_ref, masks, rs, rsend)
    project_left(ns, ps_ref, v, masks, lbuf, me.slot)

    pl.semaphore_wait(bar, len(friends))

    def first_copy(part, n):
        h, device = relays[n]
        rows = span(R_STEP, part)
        return pltpu.make_async_remote_copy(
            src_ref=rsend.at[h, rows], dst_ref=rbuf.at[me.slot, rows],
            send_sem=rs1.at[part, n], recv_sem=rr1.at[part, me.xh * 2 + me.core],
            device_id=device, device_id_type=MESH,
        )

    def second_copy(part, n):
        block = rbuf.at[pl.ds(near * 4, 4), span(R_STEP, part)]
        return pltpu.make_async_remote_copy(
            src_ref=block, dst_ref=block, send_sem=rs2.at[part, n], recv_sem=rr2.at[part, n],
            device_id=others[n], device_id_type=MESH,
        )

    def left_copy(part, n):
        piece = lbuf.at[me.slot, span(L_STEP, part)]
        return pltpu.make_async_remote_copy(
            src_ref=piece, dst_ref=piece, send_sem=ls.at[part, n], recv_sem=lr.at[part, n],
            device_id=(aways + [partner])[n], device_id_type=MESH,
        )

    def pass_on_copy(part, n):
        xh, z = froms[n]
        piece = lbuf.at[z * 4 + xh * 2 + me.core, span(L_STEP, part)]
        return pltpu.make_async_remote_copy(
            src_ref=piece, dst_ref=piece, send_sem=fs.at[part, n], recv_sem=fr.at[part, n],
            device_id=partner, device_id_type=MESH,
        )

    def start_first(part):
        rows = span(R_STEP, part)
        for n, (h, device) in enumerate(relays):
            mine = me.is_me(device)

            @pl.when(jnp.logical_not(mine))
            def _():
                first_copy(part, n).start()

            @pl.when(mine)
            def _():
                rbuf[me.slot, rows, :] = rsend[h, rows, :]

    def relay(part):
        rows = span(R_STEP, part)
        for n, device in enumerate(sources):
            @pl.when(jnp.logical_not(me.is_me(device)))
            def _():
                pltpu.make_async_remote_copy(
                    src_ref=rsend.at[0, rows], dst_ref=rbuf.at[near * 4 + n, rows],
                    send_sem=rs1.at[part, 0], recv_sem=rr1.at[part, n],
                    device_id=device, device_id_type=MESH,
                ).wait_recv()
        for n in range(3):
            second_copy(part, n).start()

    def pass_on(part):
        for n in range(7):
            left_copy(part, n).wait_recv()
            pass_on_copy(part, n).start()

    for part in range(PARTS):
        start_first(part)
        for n in range(8):
            left_copy(part, n).start()

    w_copy.wait()
    reorder_final(wv, wf, wt_ref)
    ob_ref[...] = jnp.broadcast_to(off_ref[...], (CZ, CZ)).T

    for part in range(PARTS):
        relay(part)
        pass_on(part)

    for part in range(PARTS):
        for n in range(3):
            second_copy(part, n).wait_recv()
        left_copy(part, 7).wait_recv()
        for n in range(7):
            pass_on_copy(part, n).wait_recv()
        if part == 0:
            count_pairs(lbuf, rbuf, me.core, rc_ref)
        unpack_right(rbuf, r_ref, part)
        unpack_left(lbuf, a_ref, part)

    for part in range(PARTS):
        for n, (_, device) in enumerate(relays):
            @pl.when(jnp.logical_not(me.is_me(device)))
            def _():
                first_copy(part, n).wait_send()
        for n in range(3):
            second_copy(part, n).wait_send()
        for n in range(8):
            left_copy(part, n).wait_send()
        for n in range(7):
            pass_on_copy(part, n).wait_send()


def gather(x, v, gain, ps, pt, w, off):
    vmem = pl.BlockSpec(memory_space=pltpu.VMEM)
    hbm = pl.BlockSpec(memory_space=pl.ANY)
    dma = pltpu.SemaphoreType.DMA
    return pl.pallas_call(
        gather_kernel,
        out_shape=[
            jax.ShapeDtypeStruct((ROWS * WIDTH, 128), BF16),
            jax.ShapeDtypeStruct((128, WIDTH * COLS), BF16),
            jax.ShapeDtypeStruct((CZ, WIDTH * WIDTH), BF16),
            jax.ShapeDtypeStruct((ROWS, COLS), F32),
            jax.ShapeDtypeStruct((CZ, CZ), F32),
        ],
        in_specs=[hbm, vmem, vmem, vmem, vmem, hbm, vmem],
        out_specs=[vmem] * 5,
        scratch_shapes=[
            pltpu.VMEM((SEQS, DEPTH, ROWS), BF16),
            pltpu.VMEM((WIDTH * WIDTH, CZ), BF16),
            pltpu.VMEM((WIDTH * WIDTH, CZ), F32),
            pltpu.VMEM((SEQS * ROWS, DEPTH), F32),
            pltpu.VMEM((SEQS, DEPTH, ROWS), BF16),
            pltpu.VMEM((2, WIDTH * SEQS, COLS), F32),
            pltpu.VMEM((2, R_ROWS, COLS), BF16),
            pltpu.VMEM((SLOTS, L_ROWS, 128), BF16),
            pltpu.VMEM((SLOTS, R_ROWS, COLS), BF16),
            dma((2,)),
            dma((PARTS, 4)), dma((PARTS, 4)), dma((PARTS, 3)), dma((PARTS, 3)),
            dma((PARTS, 8)), dma((PARTS, 8)), dma((PARTS, 7)), dma((PARTS, 7)),
        ],
        compiler_params=pltpu.CompilerParams(
            collective_id=0, has_side_effects=True, vmem_limit_bytes=48 * 2**20
        ),
        name="gather_factors",
    )(x, v, gain, ps, pt, w, off)


def pair_kernel(a_ref, r_ref, wt_ref, rc_ref, ob_ref, out_ref, outer, *, block):
    a = a_ref[...]
    for p in range(WIDTH // 2):
        x = jnp.dot(a, r_ref[:, p * 256 : (p + 1) * 256], preferred_element_type=F32).astype(BF16)
        for i in range(block):
            for e in range(2):
                outer[i // 2, (2 * p + e) * 32 : (2 * p + e + 1) * 32, (i % 2) * 128 : (i % 2 + 1) * 128] = x[
                    i * 32 : (i + 1) * 32, e * 128 : (e + 1) * 128
                ]
    for k in range(block // 2):
        y = jnp.dot(wt_ref[...], outer[k], preferred_element_type=F32)
        for h in range(2):
            i = 2 * k + h
            value = y[:, h * 128 : (h + 1) * 128] * rc_ref[i : i + 1, :] + ob_ref[...]
            out_ref[i] = value.astype(BF16).T


def pairs(a, r, wt, rc, ob, block=32):
    return pl.pallas_call(
        functools.partial(pair_kernel, block=block),
        grid=(ROWS // block,),
        in_specs=[
            pl.BlockSpec((block * WIDTH, 128), lambda t: (t, 0)),
            pl.BlockSpec((128, WIDTH * COLS), lambda t: (0, 0)),
            pl.BlockSpec((CZ, WIDTH * WIDTH), lambda t: (0, 0)),
            pl.BlockSpec((block, COLS), lambda t: (t, 0)),
            pl.BlockSpec((CZ, CZ), lambda t: (0, 0)),
        ],
        out_specs=pl.BlockSpec((block, COLS, CZ), lambda t: (t, 0, 0)),
        out_shape=jax.ShapeDtypeStruct((ROWS, COLS, CZ), BF16),
        scratch_shapes=[pltpu.VMEM((block // 2, WIDTH * WIDTH, 256), BF16)],
        compiler_params=pltpu.CompilerParams(vmem_limit_bytes=56 * 2**20),
        name="pair_update",
    )(a, r, wt, rc, ob)


def on_device(x, v, gain, ps, pt, w, off):
    a, r, wt, rc, ob = gather(
        x.transpose(0, 2, 1), v, gain.reshape(1, DEPTH), ps.T, pt.T, w, off.reshape(1, CZ)
    )
    return pairs(a, r, wt, rc, ob)


def solution(mesh):
    in_specs = (P("col", "row", None), P("col", "row"), P(), P(), P(), P(), P())
    return jax.shard_map(
        on_device, mesh=mesh, in_specs=in_specs, out_specs=P("row", "col", None), check_vma=False
    )
```

```python
import jax
import jax.numpy as jnp
from jax import lax
from jax.experimental import pallas as pl
from jax.experimental.pallas import tpu as pltpu
from jax.sharding import PartitionSpec as P

BF16 = jnp.bfloat16
F32 = jnp.float32
MESH = pl.DeviceIdType.MESH

SEQS = 8
ROWS = 256
COLS = 128
WIDTH = 32
DEPTH = 64
CZ = 128
SLOTS = 16
PARTS = 4
L_ROWS = 16 + ROWS // 4 * SEQS
R_ROWS = 16 + WIDTH * SEQS
HALF = ROWS // 2
STEP = 64
BLOCK = 32
L_STEP = (L_ROWS - 16) // PARTS
R_STEP = (R_ROWS - 16) // PARTS


def span(step, part):
    return pl.ds(0, 16 + step) if part == 0 else pl.ds(16 + step * part, step)


class Place:
    def __init__(self):
        self.row = lax.axis_index("row")
        self.col = lax.axis_index("col")
        self.y, self.xl = self.row // 2, self.row % 2
        chip = self.col // 2
        self.xh, self.z, self.core = chip // 4, chip % 4, self.col % 2
        self.slot = self.z * 4 + self.xh * 2 + self.core
        self.to_xh, self.to_z = self.y // 2, self.row % 4
        self.relay_y = (self.y + self.z - self.to_z + 4) % 4
        self.relay_xl = (self.xl + self.xh + self.to_xh) % 2
        self.from_y, self.from_xl = self.xh * 2 + self.z // 2, self.z % 2

        self.near_z = (self.y - self.from_y + self.z + 4) % 4
        self.near_xh = (self.xl + self.from_xl + self.xh) % 2

    def device(self, y=None, xl=None, xh=None, z=None, core=None):
        pick = lambda a, b: b if a is None else a
        y, xl, xh = pick(y, self.y), pick(xl, self.xl), pick(xh, self.xh)
        z, core = pick(z, self.z), pick(core, self.core)
        return (y * 2 + xl, (xh * 4 + z) * 2 + core)

    def is_me(self, device):
        return (device[0] == self.row) & (device[1] == self.col)


def normalise(xv, gain_ref, ns, nt):
    gain = jnp.broadcast_to(gain_ref[...], (ROWS, DEPTH)).T
    for s in range(SEQS):
        x = xv[s].astype(F32)
        center = jnp.mean(x, axis=0, keepdims=True)
        d = x - center
        spread = jnp.mean(d * d, axis=0, keepdims=True)
        normed = d * lax.rsqrt(spread + 1e-05) * gain
        nt[s] = normed.astype(BF16)
        ns[pl.ds(s * ROWS, ROWS), :] = normed.T


def masks_by_half(v):
    lane = lax.broadcasted_iota(jnp.int32, (SEQS, 128), 1)
    out = []
    for h in range(2):
        word = jnp.broadcast_to(v[:, 4 * h : 4 * h + 1], (SEQS, 128))
        for q in range(1, 4):
            word = jnp.where(lane // 32 == q, v[:, 4 * h + q : 4 * h + q + 1], word)
        out.append((lax.shift_right_logical(word, lane % 32) & 1).astype(F32))
    return out


def project_right(nt, pt_ref, masks, rs, rsend):
    for s in range(SEQS):
        y = jnp.dot(pt_ref[...], nt[s], preferred_element_type=F32)
        for h in range(2):
            rs[h, pl.ds(s, WIDTH, stride=SEQS), :] = y[:, h * COLS : (h + 1) * COLS]
    tile = jnp.concatenate(masks, axis=0).astype(BF16)
    for h in range(2):
        rsend[h, 0:16, :] = tile
        block = rs[h].reshape(WIDTH, SEQS, COLS) * masks[h][None]
        rsend[h, 16:R_ROWS, :] = block.reshape(WIDTH * SEQS, COLS).astype(BF16)


def project_left(ns, ps_ref, v, masks, lbuf, slot):
    total = None
    p = ps_ref[...].astype(F32).T.astype(BF16)
    zero = jnp.zeros_like(p)
    for a in range(4):
        n = jnp.concatenate(
            [ns[pl.ds(4 * b + a, SEQS, stride=ROWS), :] for b in range(ROWS // 4)], axis=0
        ).astype(BF16)
        wide = jnp.concatenate([p if q == a else zero for q in range(4)], axis=1)
        part = jnp.dot(n, wide, preferred_element_type=F32)
        total = part if total is None else total + part
    shift = lax.broadcasted_iota(jnp.int32, (SEQS, 128), 1) // 32
    mask = []
    for b in range(ROWS // 4):
        word = jnp.broadcast_to(v[:, b // 8 : b // 8 + 1], (SEQS, 128))
        mask.append((lax.shift_right_logical(word, shift + (b % 8) * 4) & 1).astype(F32))
    out = total * jnp.concatenate(mask, axis=0)
    lbuf[slot, 0:16, :] = jnp.concatenate(masks, axis=0).astype(BF16)
    lbuf[slot, 16:L_ROWS, :] = out.astype(BF16)


def reorder_final(wv, wf, wt):
    wf[...] = wv[...].astype(F32)
    for n in range(8):
        rows = [wf[pl.ds(4 * n + e, WIDTH, stride=WIDTH), :] for e in range(4)]
        tile = jnp.concatenate(rows, axis=0).astype(BF16).T
        wt[n // 2, :, (n % 2) * 128 : (n % 2 + 1) * 128] = tile


def unpack_left(lbuf, part, a_ref, first):
    block = lbuf[:, 16 + L_STEP * part : 16 + L_STEP * (part + 1), :].astype(F32)
    groups = L_STEP // SEQS
    block = block.reshape(SLOTS, groups, SEQS, 128)
    for b in range(groups):
        tile = block[:, b].reshape(SLOTS * SEQS, 128).astype(BF16)
        a_ref[(first * groups + b) * 128 : (first * groups + b + 1) * 128, :] = tile.T


def unpack_right(rbuf, r_ref, part):
    block = rbuf[:, 16 + R_STEP * part : 16 + R_STEP * (part + 1), :].astype(F32)
    groups = R_STEP // SEQS
    block = block.reshape(SLOTS, groups, SEQS, COLS)
    for e in range(groups):
        r_ref[part, :, e * COLS : (e + 1) * COLS] = (
            block[:, e].reshape(SLOTS * SEQS, COLS).astype(BF16)
        )


def count_pairs(lbuf, rbuf, core, rc_ref):
    mi = lbuf[:, 0:16, :].astype(F32).reshape(SLOTS, 2, SEQS, 128)
    mj = rbuf[:, 0:16, :].astype(F32).reshape(SLOTS, 2, SEQS, 128)
    first = (core == 0).astype(F32)
    cols = (mj[:, 0] * first + mj[:, 1] * (1.0 - first)).reshape(128, 128).astype(BF16)
    for h in range(2):
        rows = mi[:, h].reshape(128, 128).astype(BF16)
        counts = lax.dot_general(rows, cols, (((0,), (0,)), ((), ())), preferred_element_type=F32)
        rc_ref[pl.ds(h * 128, 128), :] = 1.0 / jnp.maximum(counts, 1.0)


def outer_part(a, r, outer, block, first, count):
    for p in range(count // 2):
        x = jnp.dot(a, r[:, p * 256 : (p + 1) * 256], preferred_element_type=F32).astype(BF16)
        for i in range(block):
            for e in range(2):
                at = (first + 2 * p + e) * WIDTH
                outer[i // 2, at : at + WIDTH, (i % 2) * COLS : (i % 2 + 1) * COLS] = x[
                    i * WIDTH : (i + 1) * WIDTH, e * COLS : (e + 1) * COLS
                ]


def finish(y, rc, ob, k, put):
    for h in range(2):
        value = y[:, h * COLS : (h + 1) * COLS] * rc[2 * k + h : 2 * k + h + 1, :] + ob
        put(2 * k + h, value.astype(BF16).T)


def first_kernel(
    x_hbm, v_hbm, gain_hbm, ps_hbm, pt_hbm, w_hbm, off_hbm,
    out_hbm, a_ref, r_ref, wt_ref, rc_ref, ob_ref,
    xv, v_ref, gain_ref, ps_ref, pt_ref, wv, off_ref,
    wf, ns, nt, rs, rsend, lbuf, rbuf, near_a, outer, acc, stage,
    in_sem, out_sem, rs1, rr1, rs2, rr2, ls, lr, fs, fr,
):
    me = Place()
    loads = [
        pltpu.make_async_copy(src, dst, in_sem.at[n])
        for n, (src, dst) in enumerate([
            (x_hbm, xv), (v_hbm, v_ref), (gain_hbm, gain_ref), (pt_hbm, pt_ref), (ps_hbm, ps_ref),
            (off_hbm, off_ref), (w_hbm, wv),
        ])
    ]
    for load in loads:
        load.start()

    shifts = [(0, 1), (0, 2), (0, 3), (1, 0), (1, 1), (1, 2), (1, 3)]
    partner = me.device(core=1 - me.core)
    across = me.device(xh=1 - me.xh)
    beside = me.device(xl=1 - me.xl)
    along_z = [me.device(z=(me.z + b) % 4) for b in (1, 2, 3)]
    along_y = [me.device(y=(me.y + d) % 4) for d in (1, 2, 3)]
    froms = [((me.xh + a) % 2, (me.z + 4 - b) % 4) for a, b in shifts]
    relays = [me.device(y=me.relay_y, xl=me.relay_xl, xh=me.to_xh, z=me.to_z, core=h) for h in range(2)]
    sources = [
        me.device(y=me.from_y, xl=me.from_xl, xh=me.near_xh, z=me.near_z, core=c) for c in range(2)
    ]
    near = me.near_z * 4 + me.near_xh * 2
    bar = pltpu.get_barrier_semaphore()
    friends = [partner, across, beside] + along_z + along_y + relays + sources
    for device in friends:
        pl.semaphore_signal(bar, inc=1, device_id=device, device_id_type=MESH)

    def remote(src, dst, send, recv, device):
        return pltpu.make_async_remote_copy(
            src_ref=src, dst_ref=dst, send_sem=send, recv_sem=recv,
            device_id=device, device_id_type=MESH,
        )

    def first_copy(part, h):
        rows = span(R_STEP, part)
        return remote(
            rsend.at[h, rows], rbuf.at[me.slot, rows],
            rs1.at[part, h], rr1.at[part, me.core], relays[h],
        )

    def second_copy(part, n):
        pair = near if n < 4 else me.near_z * 4 + (1 - me.near_xh) * 2
        block = rbuf.at[pl.ds(pair, 2), span(R_STEP, part)]
        device = beside if n == 3 else along_y[n % 4]
        return remote(block, block, rs2.at[part, n], rr2.at[part, n], device)

    def left_copy(part, n):
        slot = me.slot if n < 4 or n == 7 else me.z * 4 + (1 - me.xh) * 2 + me.core
        piece = lbuf.at[slot, span(L_STEP, part)]
        device = partner if n == 7 else across if n == 3 else along_z[n % 4]
        return remote(piece, piece, ls.at[part, n], lr.at[part, n], device)

    def pass_on_copy(part, n):
        xh, z = froms[n]
        piece = lbuf.at[z * 4 + xh * 2 + me.core, span(L_STEP, part)]
        return remote(piece, piece, fs.at[part, n], fr.at[part, n], partner)

    def start_first(part):
        rows = span(R_STEP, part)
        for h, device in enumerate(relays):
            mine = me.is_me(device)

            @pl.when(jnp.logical_not(mine))
            def _():
                first_copy(part, h).start()

            @pl.when(mine)
            def _():
                rbuf[me.slot, rows, :] = rsend[h, rows, :]

    def relay(part):
        rows = span(R_STEP, part)
        for c, device in enumerate(sources):
            @pl.when(jnp.logical_not(me.is_me(device)))
            def _():
                remote(
                    rsend.at[0, rows], rbuf.at[near + c, rows], rs1.at[part, 0], rr1.at[part, c], device
                ).wait_recv()
        for n in (3, 0, 1, 2):
            second_copy(part, n).start()

    def relay_beside(part):
        second_copy(part, 3).wait_recv()
        for n in (4, 5, 6):
            second_copy(part, n).start()

    def start_left(part):
        for n in (3, 7, 0, 1, 2):
            left_copy(part, n).start()

    def relay_across(part):
        left_copy(part, 3).wait_recv()
        for n in (4, 5, 6):
            left_copy(part, n).start()
        pass_on_copy(part, 3).start()

    def pass_on(part):
        for n in (0, 1, 2, 4, 5, 6):
            left_copy(part, n).wait_recv()
            pass_on_copy(part, n).start()

    def take_right(part):
        for n in (0, 1, 2, 4, 5, 6):
            second_copy(part, n).wait_recv()
        unpack_right(rbuf, r_ref, part)

    def wait_left(part):
        left_copy(part, 7).wait_recv()
        for n in range(7):
            pass_on_copy(part, n).wait_recv()

    def step(part, block):
        rows = L_STEP // SEQS * 128
        outer_part(near_a[block * rows : (block + 1) * rows, :], r_ref.at[part], outer, STEP, 0, 8)
        for k in range(STEP // 2):
            y = jnp.dot(wt_ref[part], outer[k], preferred_element_type=F32)
            at = block * (STEP // 2) + k
            if part == 0:
                acc[at] = y
            elif part < PARTS - 1:
                acc[at] += y
            else:
                def put(i, value):
                    stage[block * STEP + i] = value

                rc = rc_ref[block * STEP : (block + 1) * STEP, :]
                finish(acc[at] + y, rc, ob_ref[...], k, put)

    def out_copy(block):
        rows = pl.ds(block * STEP, STEP)
        return pltpu.make_async_copy(stage.at[rows], out_hbm.at[rows], out_sem.at[block])

    for load in loads[:5]:
        load.wait()
    v = v_ref[...]
    masks = masks_by_half(v)
    normalise(xv, gain_ref, ns, nt)
    project_right(nt, pt_ref, masks, rs, rsend)
    pl.semaphore_wait(bar, len(friends))
    start_first(0)
    start_first(1)
    project_left(ns, ps_ref, v, masks, lbuf, me.slot)
    start_left(0)
    start_left(1)
    start_first(2)
    start_first(3)
    start_left(2)
    start_left(3)

    for load in loads[5:]:
        load.wait()
    reorder_final(wv, wf, wt_ref)
    ob_ref[...] = jnp.broadcast_to(off_ref[...], (CZ, CZ)).T

    relay(0)
    relay_across(0)
    relay(1)
    relay_beside(0)
    relay_across(1)
    relay(2)
    relay(3)
    relay_beside(1)
    pass_on(0)
    relay_across(2)
    take_right(0)
    wait_left(0)
    unpack_left(lbuf, 0, near_a, 0)
    step(0, 0)
    relay_beside(2)
    relay_across(3)
    relay_beside(3)
    pass_on(1)
    count_pairs(lbuf, rbuf, me.core, rc_ref)
    wait_left(1)
    unpack_left(lbuf, 1, near_a, 1)
    step(0, 1)
    take_right(1)
    step(1, 0)
    pass_on(2)
    step(1, 1)
    take_right(2)
    step(2, 0)
    pass_on(3)
    step(2, 1)
    take_right(3)
    step(3, 0)
    out_copy(0).start()
    for part in (2, 3):
        wait_left(part)
        unpack_left(lbuf, part, a_ref, part - 2)
    step(3, 1)
    out_copy(1).start()

    out_copy(0).wait()
    out_copy(1).wait()
    for part in range(PARTS):
        for h, device in enumerate(relays):
            @pl.when(jnp.logical_not(me.is_me(device)))
            def _():
                first_copy(part, h).wait_send()
        for n in range(7):
            second_copy(part, n).wait_send()
        for n in range(8):
            left_copy(part, n).wait_send()
        for n in range(7):
            pass_on_copy(part, n).wait_send()


def first_half(x, v, gain, ps, pt, w, off):
    vmem = pl.BlockSpec(memory_space=pltpu.VMEM)
    hbm = pl.BlockSpec(memory_space=pltpu.HBM)
    dma = pltpu.SemaphoreType.DMA
    return pl.pallas_call(
        first_kernel,
        out_shape=[
            jax.ShapeDtypeStruct((HALF, COLS, CZ), BF16),
            jax.ShapeDtypeStruct((HALF * WIDTH, 128), BF16),
            jax.ShapeDtypeStruct((PARTS, 128, WIDTH // PARTS * COLS), BF16),
            jax.ShapeDtypeStruct((PARTS, CZ, WIDTH // PARTS * WIDTH), BF16),
            jax.ShapeDtypeStruct((ROWS, COLS), F32),
            jax.ShapeDtypeStruct((CZ, CZ), F32),
        ],
        in_specs=[hbm] * 7,
        out_specs=[hbm] + [vmem] * 5,
        scratch_shapes=[
            pltpu.VMEM((SEQS, DEPTH, ROWS), BF16),
            pltpu.VMEM((SEQS, SEQS), jnp.int32),
            pltpu.VMEM((1, DEPTH), F32),
            pltpu.VMEM((WIDTH, DEPTH), BF16),
            pltpu.VMEM((WIDTH, DEPTH), BF16),
            pltpu.VMEM((WIDTH * WIDTH, CZ), BF16),
            pltpu.VMEM((1, CZ), F32),
            pltpu.VMEM((WIDTH * WIDTH, CZ), F32),
            pltpu.VMEM((SEQS * ROWS, DEPTH), F32),
            pltpu.VMEM((SEQS, DEPTH, ROWS), BF16),
            pltpu.VMEM((2, WIDTH * SEQS, COLS), F32),
            pltpu.VMEM((2, R_ROWS, COLS), BF16),
            pltpu.VMEM((SLOTS, L_ROWS, 128), BF16),
            pltpu.VMEM((SLOTS, R_ROWS, COLS), BF16),
            pltpu.VMEM((HALF * WIDTH, 128), BF16),
            pltpu.VMEM((STEP // 2, WIDTH // PARTS * WIDTH, 2 * COLS), BF16),
            pltpu.VMEM((HALF // 2, CZ, 2 * COLS), F32),
            pltpu.VMEM((HALF, COLS, CZ), BF16),
            dma((7,)), dma((2,)),
            dma((PARTS, 2)), dma((PARTS, 2)), dma((PARTS, 7)), dma((PARTS, 7)),
            dma((PARTS, 8)), dma((PARTS, 8)), dma((PARTS, 7)), dma((PARTS, 7)),
        ],
        compiler_params=pltpu.CompilerParams(
            collective_id=0, has_side_effects=True, vmem_limit_bytes=40 * 2**20
        ),
        name="gather_and_first_half",
    )(x, v, gain, ps, pt, w, off)


def second_kernel(half_hbm, a_ref, r_ref, wt_ref, rc_ref, ob_ref, out_hbm, outer, stage, sem):
    carry = pltpu.make_async_copy(half_hbm, out_hbm.at[pl.ds(0, HALF)], sem.at[2])
    carry.start()

    def out_copy(t, slot):
        return pltpu.make_async_copy(
            stage.at[slot], out_hbm.at[pl.ds(HALF + t * BLOCK, BLOCK)], sem.at[slot]
        )

    for t in range(HALF // BLOCK):
        slot = t % 2
        rows = BLOCK * WIDTH
        a = a_ref[t * rows : (t + 1) * rows, :]
        for part in range(PARTS):
            outer_part(a, r_ref.at[part], outer, BLOCK, part * 8, 8)
        if t >= 2:
            out_copy(t - 2, slot).wait()
        rc = rc_ref[HALF + t * BLOCK : HALF + (t + 1) * BLOCK, :]
        ob = ob_ref[...]
        w = jnp.concatenate([wt_ref[part] for part in range(PARTS)], axis=1)

        def put(i, value):
            stage[slot, i] = value

        for k in range(BLOCK // 2):
            y = jnp.dot(w, outer[k], preferred_element_type=F32)
            finish(y, rc, ob, k, put)
        out_copy(t, slot).start()
    out_copy(HALF // BLOCK - 2, 0).wait()
    out_copy(HALF // BLOCK - 1, 1).wait()
    carry.wait()


def second_half(half, a, r, wt, rc, ob):
    vmem = pl.BlockSpec(memory_space=pltpu.VMEM)
    hbm = pl.BlockSpec(memory_space=pltpu.HBM)
    return pl.pallas_call(
        second_kernel,
        in_specs=[hbm] + [vmem] * 5,
        out_specs=hbm,
        out_shape=jax.ShapeDtypeStruct((ROWS, COLS, CZ), BF16),
        scratch_shapes=[
            pltpu.VMEM((BLOCK // 2, WIDTH * WIDTH, 2 * COLS), BF16),
            pltpu.VMEM((2, BLOCK, COLS, CZ), BF16),
            pltpu.SemaphoreType.DMA((3,)),
        ],
        compiler_params=pltpu.CompilerParams(vmem_limit_bytes=32 * 2**20),
        name="second_half",
    )(half, a, r, wt, rc, ob)


def on_device(x, v, gain, ps, pt, w, off):
    inputs = (x.transpose(0, 2, 1), v, gain.reshape(1, DEPTH), ps.T, pt.T, w, off.reshape(1, CZ))
    return second_half(*first_half(*[pltpu.with_memory_space_constraint(a, pltpu.HBM) for a in inputs]))


def solution(mesh):
    in_specs = (P("col", "row", None), P("col", "row"), P(), P(), P(), P(), P())
    return jax.shard_map(
        on_device, mesh=mesh, in_specs=in_specs, out_specs=P("row", "col", None), check_vma=False
    )
```

```python
import jax
import jax.numpy as jnp
from jax import lax
from jax.experimental import pallas as pl
from jax.experimental.pallas import tpu as pltpu
from jax.sharding import PartitionSpec as P

BF16 = jnp.bfloat16
F32 = jnp.float32
MESH = pl.DeviceIdType.MESH

SEQS = 8
ROWS = 256
COLS = 128
WIDTH = 32
DEPTH = 64
CZ = 128
SLOTS = 16
PARTS = 4
L_ROWS = 16 + ROWS // 4 * SEQS
R_ROWS = 16 + WIDTH * SEQS
HALF = ROWS // 2
STEP = 64
BLOCK = 32
L_STEP = (L_ROWS - 16) // PARTS
R_STEP = (R_ROWS - 16) // PARTS


def span(step, part):
    return pl.ds(0, 16 + step) if part == 0 else pl.ds(16 + step * part, step)


class Place:
    def __init__(self):
        self.row = lax.axis_index("row")
        self.col = lax.axis_index("col")
        self.y, self.xl = self.row // 2, self.row % 2
        chip = self.col // 2
        self.xh, self.z, self.core = chip // 4, chip % 4, self.col % 2
        self.slot = self.z * 4 + self.xh * 2 + self.core
        self.to_xh, self.to_z = self.y // 2, self.row % 4
        turn, shift = self.turn(self.y, self.xl)
        self.relay_y = (self.y + turn * (self.z - self.to_z + 4) + shift) % 4
        self.relay_xl = (self.xl + self.xh + self.to_xh) % 2
        self.from_y, self.from_xl = self.xh * 2 + self.z // 2, self.z % 2

        turn, shift = self.turn(self.from_y, self.from_xl)
        self.near_z = (self.z + turn * (self.y - self.from_y - shift + 8)) % 4
        self.near_xh = (self.xl + self.from_xl + self.xh) % 2

    def turn(self, y, xl):
        return 1 + 2 * (y % 2), xl * (3 - 2 * (y % 2))

    def device(self, y=None, xl=None, xh=None, z=None, core=None):
        pick = lambda a, b: b if a is None else a
        y, xl, xh = pick(y, self.y), pick(xl, self.xl), pick(xh, self.xh)
        z, core = pick(z, self.z), pick(core, self.core)
        return (y * 2 + xl, (xh * 4 + z) * 2 + core)

    def is_me(self, device):
        return (device[0] == self.row) & (device[1] == self.col)


def normalise(xv, gain_ref, ns, nt):
    gain = jnp.broadcast_to(gain_ref[...], (ROWS, DEPTH)).T
    for s in range(SEQS):
        x = xv[s].astype(F32)
        center = jnp.mean(x, axis=0, keepdims=True)
        d = x - center
        spread = jnp.mean(d * d, axis=0, keepdims=True)
        normed = d * lax.rsqrt(spread + 1e-05) * gain
        nt[s] = normed.astype(BF16)
        ns[pl.ds(s * ROWS, ROWS), :] = normed.T


def masks_by_half(v):
    lane = lax.broadcasted_iota(jnp.int32, (SEQS, 128), 1)
    out = []
    for h in range(2):
        word = jnp.broadcast_to(v[:, 4 * h : 4 * h + 1], (SEQS, 128))
        for q in range(1, 4):
            word = jnp.where(lane // 32 == q, v[:, 4 * h + q : 4 * h + q + 1], word)
        out.append((lax.shift_right_logical(word, lane % 32) & 1).astype(F32))
    return out


def project_right(nt, pt_ref, masks, rs, rsend):
    for s in range(SEQS):
        y = jnp.dot(pt_ref[...], nt[s], preferred_element_type=F32)
        for h in range(2):
            rs[h, pl.ds(s, WIDTH, stride=SEQS), :] = y[:, h * COLS : (h + 1) * COLS]
    tile = jnp.concatenate(masks, axis=0).astype(BF16)
    for h in range(2):
        rsend[h, 0:16, :] = tile
        block = rs[h].reshape(WIDTH, SEQS, COLS) * masks[h][None]
        rsend[h, 16:R_ROWS, :] = block.reshape(WIDTH * SEQS, COLS).astype(BF16)


def project_left(ns, ps_ref, v, masks, lbuf, slot):
    total = None
    p = ps_ref[...].astype(F32).T.astype(BF16)
    zero = jnp.zeros_like(p)
    for a in range(4):
        n = jnp.concatenate(
            [ns[pl.ds(4 * b + a, SEQS, stride=ROWS), :] for b in range(ROWS // 4)], axis=0
        ).astype(BF16)
        wide = jnp.concatenate([p if q == a else zero for q in range(4)], axis=1)
        part = jnp.dot(n, wide, preferred_element_type=F32)
        total = part if total is None else total + part
    shift = lax.broadcasted_iota(jnp.int32, (SEQS, 128), 1) // 32
    mask = []
    for b in range(ROWS // 4):
        word = jnp.broadcast_to(v[:, b // 8 : b // 8 + 1], (SEQS, 128))
        mask.append((lax.shift_right_logical(word, shift + (b % 8) * 4) & 1).astype(F32))
    out = total * jnp.concatenate(mask, axis=0)
    lbuf[slot, 0:16, :] = jnp.concatenate(masks, axis=0).astype(BF16)
    lbuf[slot, 16:L_ROWS, :] = out.astype(BF16)


def reorder_final(wv, wf, wt):
    wf[...] = wv[...].astype(F32)
    for n in range(8):
        rows = [wf[pl.ds(4 * n + e, WIDTH, stride=WIDTH), :] for e in range(4)]
        tile = jnp.concatenate(rows, axis=0).astype(BF16).T
        wt[n // 2, :, (n % 2) * 128 : (n % 2 + 1) * 128] = tile


def unpack_left(lbuf, part, a_ref, first):
    block = lbuf[:, 16 + L_STEP * part : 16 + L_STEP * (part + 1), :].astype(F32)
    groups = L_STEP // SEQS
    block = block.reshape(SLOTS, groups, SEQS, 128)
    for b in range(groups):
        tile = block[:, b].reshape(SLOTS * SEQS, 128).astype(BF16)
        a_ref[(first * groups + b) * 128 : (first * groups + b + 1) * 128, :] = tile.T


def unpack_right(rbuf, r_ref, part):
    block = rbuf[:, 16 + R_STEP * part : 16 + R_STEP * (part + 1), :].astype(F32)
    groups = R_STEP // SEQS
    block = block.reshape(SLOTS, groups, SEQS, COLS)
    for e in range(groups):
        r_ref[part, :, e * COLS : (e + 1) * COLS] = (
            block[:, e].reshape(SLOTS * SEQS, COLS).astype(BF16)
        )


def count_pairs(lbuf, rbuf, core, rc_ref):
    mi = lbuf[:, 0:16, :].astype(F32).reshape(SLOTS, 2, SEQS, 128)
    mj = rbuf[:, 0:16, :].astype(F32).reshape(SLOTS, 2, SEQS, 128)
    first = (core == 0).astype(F32)
    cols = (mj[:, 0] * first + mj[:, 1] * (1.0 - first)).reshape(128, 128).astype(BF16)
    for h in range(2):
        rows = mi[:, h].reshape(128, 128).astype(BF16)
        counts = lax.dot_general(rows, cols, (((0,), (0,)), ((), ())), preferred_element_type=F32)
        rc_ref[pl.ds(h * 128, 128), :] = 1.0 / jnp.maximum(counts, 1.0)


def outer_part(a, r, outer, block, first, count):
    for p in range(count // 2):
        x = jnp.dot(a, r[:, p * 256 : (p + 1) * 256], preferred_element_type=F32).astype(BF16)
        for i in range(block):
            for e in range(2):
                at = (first + 2 * p + e) * WIDTH
                outer[i // 2, at : at + WIDTH, (i % 2) * COLS : (i % 2 + 1) * COLS] = x[
                    i * WIDTH : (i + 1) * WIDTH, e * COLS : (e + 1) * COLS
                ]


def finish(y, rc, ob, k, put):
    for h in range(2):
        value = y[:, h * COLS : (h + 1) * COLS] * rc[2 * k + h : 2 * k + h + 1, :] + ob
        put(2 * k + h, value.astype(BF16).T)


def first_kernel(
    x_hbm, v_hbm, gain_hbm, ps_hbm, pt_hbm, w_hbm, off_hbm,
    half_ref, a_ref, r_ref, wt_ref, rc_ref, ob_ref,
    xv, v_ref, gain_ref, ps_ref, pt_ref, wv, off_ref,
    wf, ns, nt, rs, rsend, lbuf, rbuf, near_a, outer, acc,
    in_sem, rs1, rr1, rs2, rr2, ls, lr, fs, fr,
):
    me = Place()
    loads = [
        pltpu.make_async_copy(src, dst, in_sem.at[n])
        for n, (src, dst) in enumerate([
            (x_hbm, xv), (v_hbm, v_ref), (gain_hbm, gain_ref), (pt_hbm, pt_ref), (ps_hbm, ps_ref),
            (off_hbm, off_ref), (w_hbm, wv),
        ])
    ]
    for load in loads:
        load.start()

    shifts = [(0, 1), (0, 2), (0, 3), (1, 0), (1, 1), (1, 2), (1, 3)]
    partner = me.device(core=1 - me.core)
    across = me.device(xh=1 - me.xh)
    beside = me.device(xl=1 - me.xl)
    along_z = [me.device(z=(me.z + b) % 4) for b in (1, 2, 3)]
    along_y = [me.device(y=(me.y + d) % 4) for d in (1, 2, 3)]
    froms = [((me.xh + a) % 2, (me.z + 4 - b) % 4) for a, b in shifts]
    relays = [me.device(y=me.relay_y, xl=me.relay_xl, xh=me.to_xh, z=me.to_z, core=h) for h in range(2)]
    sources = [
        me.device(y=me.from_y, xl=me.from_xl, xh=me.near_xh, z=me.near_z, core=c) for c in range(2)
    ]
    near = me.near_z * 4 + me.near_xh * 2
    bar = pltpu.get_barrier_semaphore()
    friends = [partner, across, beside] + along_z + along_y + relays + sources
    for device in friends:
        pl.semaphore_signal(bar, inc=1, device_id=device, device_id_type=MESH)

    def remote(src, dst, send, recv, device):
        return pltpu.make_async_remote_copy(
            src_ref=src, dst_ref=dst, send_sem=send, recv_sem=recv,
            device_id=device, device_id_type=MESH,
        )

    def first_copy(part, h):
        rows = span(R_STEP, part)
        return remote(
            rsend.at[h, rows], rbuf.at[me.slot, rows],
            rs1.at[part, h], rr1.at[part, me.core], relays[h],
        )

    def second_copy(part, n):
        pair = near if n < 4 else me.near_z * 4 + (1 - me.near_xh) * 2
        block = rbuf.at[pl.ds(pair, 2), span(R_STEP, part)]
        device = beside if n == 3 else along_y[n % 4]
        return remote(block, block, rs2.at[part, n], rr2.at[part, n], device)

    def left_copy(part, n):
        slot = me.slot if n < 4 or n == 7 else me.z * 4 + (1 - me.xh) * 2 + me.core
        piece = lbuf.at[slot, span(L_STEP, part)]
        device = partner if n == 7 else across if n == 3 else along_z[n % 4]
        return remote(piece, piece, ls.at[part, n], lr.at[part, n], device)

    def pass_on_copy(part, n):
        xh, z = froms[n]
        piece = lbuf.at[z * 4 + xh * 2 + me.core, span(L_STEP, part)]
        return remote(piece, piece, fs.at[part, n], fr.at[part, n], partner)

    def start_first(part):
        rows = span(R_STEP, part)
        for h, device in enumerate(relays):
            mine = me.is_me(device)

            @pl.when(jnp.logical_not(mine))
            def _():
                first_copy(part, h).start()

            @pl.when(mine)
            def _():
                rbuf[me.slot, rows, :] = rsend[h, rows, :]

    def relay(part):
        rows = span(R_STEP, part)
        for c, device in enumerate(sources):
            @pl.when(jnp.logical_not(me.is_me(device)))
            def _():
                remote(
                    rsend.at[0, rows], rbuf.at[near + c, rows], rs1.at[part, 0], rr1.at[part, c], device
                ).wait_recv()
        for n in (3, 0, 1, 2):
            second_copy(part, n).start()

    def relay_beside(part):
        second_copy(part, 3).wait_recv()
        for n in (4, 5, 6):
            second_copy(part, n).start()

    def start_left(part):
        left_copy(part, 3).start()
        left_copy(part, 7).start()

    def left_z(part):
        for n in range(3):
            left_copy(part, n).start()

    def relay_across(part):
        left_copy(part, 3).wait_recv()
        for n in (4, 5, 6):
            left_copy(part, n).start()
        pass_on_copy(part, 3).start()

    def pass_on(part):
        for n in (0, 1, 2, 4, 5, 6):
            left_copy(part, n).wait_recv()
            pass_on_copy(part, n).start()

    def take_right(part):
        for n in (0, 1, 2, 4, 5, 6):
            second_copy(part, n).wait_recv()
        unpack_right(rbuf, r_ref, part)

    def wait_left(part):
        left_copy(part, 7).wait_recv()
        for n in range(7):
            pass_on_copy(part, n).wait_recv()

    def step(part, block):
        rows = L_STEP // SEQS * 128
        outer_part(near_a[block * rows : (block + 1) * rows, :], r_ref.at[part], outer, STEP, 0, 8)
        for k in range(STEP // 2):
            y = jnp.dot(wt_ref[part], outer[k], preferred_element_type=F32)
            at = block * (STEP // 2) + k
            if part == 0:
                acc[at] = y
            elif part < PARTS - 1:
                acc[at] += y
            else:
                def put(i, value):
                    half_ref[block * STEP + i] = value

                rc = rc_ref[block * STEP : (block + 1) * STEP, :]
                finish(acc[at] + y, rc, ob_ref[...], k, put)

    for load in loads[:5]:
        load.wait()
    v = v_ref[...]
    masks = masks_by_half(v)
    normalise(xv, gain_ref, ns, nt)
    project_right(nt, pt_ref, masks, rs, rsend)
    pl.semaphore_wait(bar, len(friends))
    start_first(0)
    start_first(1)
    project_left(ns, ps_ref, v, masks, lbuf, me.slot)
    for part in (0, 1):
        start_left(part)
        left_z(part)
    start_first(2)
    start_first(3)
    for part in (2, 3):
        start_left(part)
        left_z(part)

    for load in loads[5:]:
        load.wait()
    reorder_final(wv, wf, wt_ref)
    ob_ref[...] = jnp.broadcast_to(off_ref[...], (CZ, CZ)).T

    relay(0)
    relay_across(0)
    relay(1)
    relay_beside(0)
    relay_across(1)
    relay(2)
    relay(3)
    relay_beside(1)
    pass_on(0)
    relay_across(2)
    take_right(0)
    wait_left(0)
    unpack_left(lbuf, 0, near_a, 0)
    step(0, 0)
    relay_beside(2)
    relay_across(3)
    relay_beside(3)
    pass_on(1)
    count_pairs(lbuf, rbuf, me.core, rc_ref)
    take_right(1)
    step(1, 0)
    wait_left(1)
    unpack_left(lbuf, 1, near_a, 1)
    step(0, 1)
    step(1, 1)
    take_right(2)
    pass_on(2)
    step(2, 0)
    pass_on(3)
    step(2, 1)
    take_right(3)
    step(3, 0)
    wait_left(2)
    unpack_left(lbuf, 2, a_ref, 0)
    step(3, 1)
    wait_left(3)
    unpack_left(lbuf, 3, a_ref, 1)

    for part in range(PARTS):
        for h, device in enumerate(relays):
            @pl.when(jnp.logical_not(me.is_me(device)))
            def _():
                first_copy(part, h).wait_send()
        for n in range(7):
            second_copy(part, n).wait_send()
        for n in range(8):
            left_copy(part, n).wait_send()
        for n in range(7):
            pass_on_copy(part, n).wait_send()


def first_half(x, v, gain, ps, pt, w, off):
    vmem = pl.BlockSpec(memory_space=pltpu.VMEM)
    hbm = pl.BlockSpec(memory_space=pltpu.HBM)
    dma = pltpu.SemaphoreType.DMA
    return pl.pallas_call(
        first_kernel,
        out_shape=[
            jax.ShapeDtypeStruct((HALF, COLS, CZ), BF16),
            jax.ShapeDtypeStruct((HALF * WIDTH, 128), BF16),
            jax.ShapeDtypeStruct((PARTS, 128, WIDTH // PARTS * COLS), BF16),
            jax.ShapeDtypeStruct((PARTS, CZ, WIDTH // PARTS * WIDTH), BF16),
            jax.ShapeDtypeStruct((ROWS, COLS), F32),
            jax.ShapeDtypeStruct((CZ, CZ), F32),
        ],
        in_specs=[hbm] * 7,
        out_specs=[vmem] * 6,
        scratch_shapes=[
            pltpu.VMEM((SEQS, DEPTH, ROWS), BF16),
            pltpu.VMEM((SEQS, SEQS), jnp.int32),
            pltpu.VMEM((1, DEPTH), F32),
            pltpu.VMEM((WIDTH, DEPTH), BF16),
            pltpu.VMEM((WIDTH, DEPTH), BF16),
            pltpu.VMEM((WIDTH * WIDTH, CZ), BF16),
            pltpu.VMEM((1, CZ), F32),
            pltpu.VMEM((WIDTH * WIDTH, CZ), F32),
            pltpu.VMEM((SEQS * ROWS, DEPTH), F32),
            pltpu.VMEM((SEQS, DEPTH, ROWS), BF16),
            pltpu.VMEM((2, WIDTH * SEQS, COLS), F32),
            pltpu.VMEM((2, R_ROWS, COLS), BF16),
            pltpu.VMEM((SLOTS, L_ROWS, 128), BF16),
            pltpu.VMEM((SLOTS, R_ROWS, COLS), BF16),
            pltpu.VMEM((HALF * WIDTH, 128), BF16),
            pltpu.VMEM((STEP // 2, WIDTH // PARTS * WIDTH, 2 * COLS), BF16),
            pltpu.VMEM((HALF // 2, CZ, 2 * COLS), F32),
            dma((7,)),
            dma((PARTS, 2)), dma((PARTS, 2)), dma((PARTS, 7)), dma((PARTS, 7)),
            dma((PARTS, 8)), dma((PARTS, 8)), dma((PARTS, 7)), dma((PARTS, 7)),
        ],
        compiler_params=pltpu.CompilerParams(
            collective_id=0, has_side_effects=True, vmem_limit_bytes=40 * 2**20
        ),
        name="gather_and_first_half",
    )(x, v, gain, ps, pt, w, off)


def second_kernel(half_ref, a_ref, r_ref, wt_ref, rc_ref, ob_ref, out_hbm, outer, stage, sem):
    carry = pltpu.make_async_copy(half_ref, out_hbm.at[pl.ds(0, HALF)], sem.at[2])
    carry.start()

    def out_copy(t, slot):
        return pltpu.make_async_copy(
            stage.at[slot], out_hbm.at[pl.ds(HALF + t * BLOCK, BLOCK)], sem.at[slot]
        )

    for t in range(HALF // BLOCK):
        slot = t % 2
        rows = BLOCK * WIDTH
        a = a_ref[t * rows : (t + 1) * rows, :]
        for part in range(PARTS):
            outer_part(a, r_ref.at[part], outer, BLOCK, part * 8, 8)
        if t >= 2:
            out_copy(t - 2, slot).wait()
        rc = rc_ref[HALF + t * BLOCK : HALF + (t + 1) * BLOCK, :]
        ob = ob_ref[...]
        w = jnp.concatenate([wt_ref[part] for part in range(PARTS)], axis=1)

        def put(i, value):
            stage[slot, i] = value

        for k in range(BLOCK // 2):
            y = jnp.dot(w, outer[k], preferred_element_type=F32)
            finish(y, rc, ob, k, put)
        out_copy(t, slot).start()
    out_copy(HALF // BLOCK - 2, 0).wait()
    out_copy(HALF // BLOCK - 1, 1).wait()
    carry.wait()


def second_half(half, a, r, wt, rc, ob):
    vmem = pl.BlockSpec(memory_space=pltpu.VMEM)
    hbm = pl.BlockSpec(memory_space=pltpu.HBM)
    return pl.pallas_call(
        second_kernel,
        in_specs=[vmem] * 6,
        out_specs=hbm,
        out_shape=jax.ShapeDtypeStruct((ROWS, COLS, CZ), BF16),
        scratch_shapes=[
            pltpu.VMEM((BLOCK // 2, WIDTH * WIDTH, 2 * COLS), BF16),
            pltpu.VMEM((2, BLOCK, COLS, CZ), BF16),
            pltpu.SemaphoreType.DMA((3,)),
        ],
        compiler_params=pltpu.CompilerParams(vmem_limit_bytes=32 * 2**20),
        name="second_half",
    )(half, a, r, wt, rc, ob)


def on_device(x, v, gain, ps, pt, w, off):
    inputs = (x.transpose(0, 2, 1), v, gain.reshape(1, DEPTH), ps.T, pt.T, w, off.reshape(1, CZ))
    return second_half(*first_half(*[pltpu.with_memory_space_constraint(a, pltpu.HBM) for a in inputs]))


def solution(mesh):
    in_specs = (P("col", "row", None), P("col", "row"), P(), P(), P(), P(), P())
    return jax.shard_map(
        on_device, mesh=mesh, in_specs=in_specs, out_specs=P("row", "col", None), check_vma=False
    )
```
